128 devices in a mesh: tt: 8 (over z_lo, x), sv: 16 (over z_hi, y, core).
Axes of the slice: x: 4, y: 4, z: 4 (z_hi: 2, z_lo: 2; z = z_hi * 2 + z_lo), core: 2. Of those that a mesh axis runs over, the one named last changes fastest.
Arguments:
- teacher_hidden: bfloat16 [256, 16384], P(None, 'sv'), may hold values from -620 to 620
- teacher_head: bfloat16 [16384, 65536], P('sv', 'tt'), may hold values from -0.046875 to 0.046875
- student_hidden: bfloat16 [256, 4096], P(('tt', 'sv')), may hold values from -42 to 42
- student_head: bfloat16 [4096, 65536], P(None, ('tt', 'sv')), may hold values from -1.5 to 1.5
- targets: int32 [256], replicated, may hold values from 0 to 65535
Outputs:
- loss: float32 [], replicated
- head_grad: bfloat16 [4096, 65536], P(None, ('tt', 'sv'))
- hidden_grad: float32 [256, 4096], P(('tt', 'sv'))
The draws below stay inside these ranges and needn't reach their ends.
All inputs are finite; a program needn't handle non-finite values.
Results may differ from the reference program's by a relative error of at most 0.0038.
Values may be sent and summed in bfloat16 or wider, within the bound.
No kernel may reach another device: no remote copies, remote signals or barrier semaphores. Data moves between devices by JAX's collectives and lax.ppermute only.
A program may use at most 128 MiB of HBM per device.

```python
import math
import jax
import jax.numpy as jnp
from jax import lax

DT = 16384
DS = 4096
V = 65536
TOKENS = 256


def row_factors(key, rows, low, high, boost):
    key_scale, key_boost = jax.random.split(key)
    scale = jnp.exp(jax.random.uniform(key_scale, (rows, 1), jnp.float32, math.log(low), math.log(high)))
    picks = jax.random.randint(key_boost, (rows, 1), 0, 16)
    return scale * jnp.where(picks == 0, boost, 1.0)


def draw_teacher_hidden(key, part):
    key = jax.random.fold_in(key, 11)
    key_base, key_rows = jax.random.split(key)
    base = jnp.clip(jax.random.normal(key_base, (TOKENS, DT), jnp.float32), -6.0, 6.0)
    factors = row_factors(key_rows, TOKENS, 3.0, 30.0, 1.0)
    return (base * factors).astype(jnp.bfloat16)


def draw_student_hidden(key, part):
    key = jax.random.fold_in(key, 23)
    key_base, key_rows = jax.random.split(key)
    base = jnp.clip(jax.random.normal(key_base, (TOKENS, DS), jnp.float32), -6.0, 6.0)
    factors = row_factors(key_rows, TOKENS, 0.2, 2.0, 1.0)
    return (base * factors).astype(jnp.bfloat16)


def touch_ends(array, key, low, high):
    longest = array.shape.index(max(array.shape))
    spots = []
    for shift in (0, 1):
        where = [jax.random.randint(jax.random.fold_in(key, axis), (), 0, length) for axis, length in enumerate(array.shape)]
        where[longest] = (where[longest] + shift) % array.shape[longest]
        spots.append(tuple(where))
    return array.at[spots[0]].set(low).at[spots[1]].set(high)


def block_scale(stream_key, extent, pieces, smallest, high):
    loudness = 1.0
    for axis_at, parts in pieces:
        steps = jax.random.uniform(jax.random.fold_in(jax.random.fold_in(stream_key, 6), axis_at), (parts,), jnp.float32, smallest / len(pieces), high / len(pieces))
        loudness = loudness * jnp.repeat(jnp.exp(steps), extent[axis_at] // parts).reshape((-1,) + (1,) * (len(extent) - 1 - axis_at))
    return loudness


def scatter_about(own_key, shape, width, limit, cuts=(), dtype=jnp.bfloat16):
    result = width * jax.random.normal(own_key, shape, jnp.float32)
    if cuts:
        result = result * block_scale(own_key, shape, cuts, -0.22, 0.18)
    return jnp.clip(result, -limit, limit).astype(dtype)


def setup_inputs(seed: int = 0) -> dict:
    arg_keys = jax.random.split(jax.random.key(seed), 6)
    teacher_hidden = draw_teacher_hidden(jax.random.fold_in(arg_keys[5], 71), 0)
    teacher_head = scatter_about(arg_keys[1], (DT, V), DT ** -0.5, 0.046875, ((0, 16), (1, 8)))
    student_hidden = draw_student_hidden(jax.random.fold_in(arg_keys[5], 71), 0)
    student_head = scatter_about(arg_keys[3], (DS, V), 0.25, 1.5, ((1, 128),))
    targets = touch_ends(jax.random.randint(arg_keys[4], (TOKENS,), 0, V), jax.random.fold_in(arg_keys[4], 1), 0, V - 1).astype(jnp.int32)
    return {"teacher_hidden": teacher_hidden, "teacher_head": teacher_head, "student_hidden": student_hidden, "student_head": student_head, "targets": targets}


ce_weight = 0.5


def log_softmax_rows(logits):
    top = jnp.max(logits, axis=1, keepdims=True)
    return logits - (top + jnp.log(jnp.sum(jnp.exp(logits - top), axis=1, keepdims=True)))


def reference(teacher_hidden, teacher_head, student_hidden, student_head, targets):
    tokens = teacher_hidden.shape[0]
    logits_t = jnp.dot(teacher_hidden, teacher_head, preferred_element_type=jnp.float32)
    log_t = log_softmax_rows(logits_t)
    rounded = lax.optimization_barrier(jnp.exp(log_t).astype(jnp.bfloat16))
    probs = rounded.astype(jnp.float32)
    entropy = jnp.sum(probs * log_t)
    logits_s = jnp.dot(student_hidden, student_head, preferred_element_type=jnp.float32)
    top = jnp.max(logits_s, axis=1)
    norm_s = top + jnp.log(jnp.sum(jnp.exp(logits_s - top[:, None]), axis=1))
    columns = lax.broadcasted_iota(jnp.int32, (1, logits_s.shape[1]), 1)
    hit = (columns == targets.astype(jnp.int32)[:, None]).astype(jnp.float32)
    cross = jnp.sum(probs * logits_s, axis=1)
    mass = jnp.sum(probs, axis=1)
    picked = jnp.sum(hit * logits_s, axis=1)
    loss = (entropy - jnp.sum(cross - mass * norm_s) + ce_weight * jnp.sum(norm_s - picked)) / tokens
    probs_s = jnp.exp(logits_s - norm_s[:, None])
    grad_logits = ((mass + ce_weight)[:, None] * probs_s - probs - ce_weight * hit).astype(jnp.bfloat16)
    head_grad = jnp.dot(student_hidden.T, grad_logits, preferred_element_type=jnp.float32).astype(jnp.bfloat16)
    hidden_grad = jnp.dot(grad_logits, student_head.T, preferred_element_type=jnp.float32)
    return loss, head_grad, hidden_grad
```

```python
import jax
import jax.numpy as jnp
from jax import lax
from jax.experimental import pallas as pl
from jax.experimental.pallas import tpu as pltpu
from jax.sharding import Mesh, PartitionSpec as P

ce_weight = 0.5
f16, f32, bf16, i16 = jnp.float16, jnp.float32, jnp.bfloat16, jnp.int16
axes = ("zl", "x", "zh", "y", "c")
sizes = (2, 4, 2, 4, 2)
grad_scale = 4096.0


def shift(value, axis, step):
    size = sizes[axes.index(axis)]
    return lax.ppermute(value, axis, [((i + step) % size, i) for i in range(size)])


def send(value, axis, step):
    size = sizes[axes.index(axis)]
    return lax.ppermute(value, axis, [(i, (i + step) % size) for i in range(size)])


def cross_z(value, across):
    pairs = [(i, i ^ (2 * ("zl" in across) + ("zh" in across))) for i in range(4)]
    return lax.ppermute(value, ("zl", "zh"), pairs)


def ring_pair(axis, first):
    return [(0, 1), (1, 0), (2, 3), (3, 2)] if first else [(0, 3), (3, 0), (1, 2), (2, 1)]


def merge(a, b):
    top_t = jnp.maximum(a[0], b[0])
    top_s = jnp.maximum(a[4], b[4])
    at, bt = jnp.exp(a[0] - top_t), jnp.exp(b[0] - top_t)
    as_, bs = jnp.exp(a[4] - top_s), jnp.exp(b[4] - top_s)
    return jnp.stack(
        [
            top_t,
            a[1] * at + b[1] * bt,
            a[2] * at + b[2] * bt,
            a[3] * at + b[3] * bt,
            top_s,
            a[5] * as_ + b[5] * bs,
            a[6] + b[6],
            a[7] + b[7],
        ]
    )


def merge_all(stats):
    stats = merge(stats, send(stats, "c", 1))
    for axis in ("x", "y"):
        for first in (True, False):
            stats = merge(stats, lax.ppermute(stats, axis, ring_pair(axis, first)))
    one, two, three = [cross_z(stats, r) for r in (("zl",), ("zh",), ("zl", "zh"))]
    return merge(merge(stats, one), merge(two, three))


def row_code(top):
    return jnp.ceil(8.0 * jnp.log2(jnp.maximum(top, 1e-30)) + 0.01)


def step_of(code):
    return jnp.exp2(code * 0.125) * (1.0 / 32000.0)


def top_of(blocks):
    top = jnp.max(jnp.abs(blocks[0]), axis=1, keepdims=True)
    for block in blocks[1:]:
        top = jnp.maximum(top, jnp.max(jnp.abs(block), axis=1, keepdims=True))
    return top


def put(ref, blocks, code):
    inverse = 1.0 / step_of(code)
    for i, block in enumerate(blocks):
        ref[:, i * 512 : (i + 1) * 512] = jnp.round(block * inverse).astype(i16)
    n = len(blocks) * 512
    ref[:, n : n + 128] = jnp.broadcast_to(code, (code.shape[0], 128)).astype(i16)


def take(ref, i, count):
    step = step_of(ref[:, count * 512 : count * 512 + 128].astype(f32)[:, :1])
    return ref[:, i * 512 : (i + 1) * 512].astype(f32) * step


def cost(us):
    return pl.CostEstimate(flops=int(us * 1e9), bytes_accessed=int(us * 2.5e6), transcendentals=0)


anywhere = pl.BlockSpec(memory_space=pl.ANY)
in_vmem = pl.BlockSpec(memory_space=pltpu.VMEM)
in_smem = pl.BlockSpec(memory_space=pltpu.SMEM)


def fetch_blocks(order_ref, head_ref, held, sems):
    copies = []
    for j in range(held.shape[0]):
        columns = pl.ds(pl.multiple_of(order_ref[j] * 512, 512), 512)
        copies.append(pltpu.make_async_copy(head_ref.at[:, columns], held.at[j], sems.at[j]))
        copies[-1].start()
    return copies


def far_products(hidden, head, order):
    count = order.shape[0]
    rows, depth = hidden.shape

    def kernel(order_ref, hidden_ref, head_ref, out_ref, held, sems):
        copies = fetch_blocks(order_ref, head_ref, held, sems)
        for j in range(count):
            copies[j].wait()
            block = jnp.dot(hidden_ref[...], held[j], preferred_element_type=f32)
            put(out_ref.at[j], [block], row_code(top_of([block])))

    return pl.pallas_call(
        kernel,
        in_specs=[in_smem, in_vmem, anywhere],
        out_specs=in_vmem,
        out_shape=jax.ShapeDtypeStruct((count, rows, 640), i16),
        scratch_shapes=[pltpu.VMEM((count, depth, 512), bf16), pltpu.SemaphoreType.DMA((count,))],
        compiler_params=pltpu.CompilerParams(vmem_limit_bytes=50 << 20),
        cost_estimate=cost(6),
    )(order, hidden, head)


def first_products(hidden, head, order):
    count = order.shape[0]
    rows, depth = hidden.shape

    def kernel(order_ref, hidden_ref, head_ref, out_ref, held, sems):
        copies = fetch_blocks(order_ref, head_ref, held, sems)
        for j in range(count):
            copies[j].wait()
            out_ref[j] = jnp.dot(hidden_ref[...], held[j], preferred_element_type=f32)

    return pl.pallas_call(
        kernel,
        in_specs=[in_smem, in_vmem, anywhere],
        out_specs=in_vmem,
        out_shape=jax.ShapeDtypeStruct((count, rows, 512), f32),
        scratch_shapes=[pltpu.VMEM((count, depth, 512), bf16), pltpu.SemaphoreType.DMA((count,))],
        compiler_params=pltpu.CompilerParams(vmem_limit_bytes=50 << 20),
        cost_estimate=cost(4),
    )(order, hidden, head)


def own_products(hidden, head, order, first, other, ready):
    rows, depth = hidden.shape
    half = rows // 2

    def kernel(order_ref, hidden_ref, head_ref, first_ref, other_ref, *refs):
        a1, a2, a3, b1, keep_a, keep_b, held, sums, sems = refs[len(ready) :]
        copies = fetch_blocks(order_ref, head_ref, held, sems)
        up, low = jnp.zeros((half, 1), f32), jnp.zeros((half, 1), f32)
        for j in range(8):
            if j < 4:
                block = first_ref[j]
            else:
                copies[j - 4].wait()
                block = jnp.dot(hidden_ref[...], held[j - 4], preferred_element_type=f32)
            block += take(other_ref.at[j], 0, 1)
            top = jnp.max(jnp.abs(block), axis=1, keepdims=True)
            if j % 4:
                sums[j, :half] = block[:half]
                up = jnp.maximum(up, top[:half])
            else:
                keep_a[:, j * 128 : j * 128 + 512] = block[:half]
            if j >= 4:
                sums[j, half:] = block[half:]
                low = jnp.maximum(low, top[half:])
            else:
                keep_b[:, j * 512 : j * 512 + 512] = block[half:]
        code = row_code(up)
        for d, ref in ((1, a1), (2, a2), (3, a3)):
            put(ref, [sums[d, :half], sums[4 + d, :half]], code)
        put(b1, [sums[4 + d, half:] for d in range(4)], row_code(low))

    outs = [(half, 1152, i16)] * 3 + [(half, 2176, i16), (half, 1024, f32), (half, 2048, f32)]
    return pl.pallas_call(
        kernel,
        in_specs=[in_smem, in_vmem, anywhere, in_vmem, in_vmem] + [anywhere] * len(ready),
        out_specs=[in_vmem] * len(outs),
        out_shape=[jax.ShapeDtypeStruct((m, n), d) for m, n, d in outs],
        scratch_shapes=[
            pltpu.VMEM((4, depth, 512), bf16),
            pltpu.VMEM((8, rows, 512), f32),
            pltpu.SemaphoreType.DMA((4,)),
        ],
        compiler_params=pltpu.CompilerParams(vmem_limit_bytes=50 << 20),
        cost_estimate=cost(7),
    )(order, hidden, head, first, other, *ready)


def whole_call(kernel, ins, outs, ready=(), scratch=(), us=0.5):
    total = sum(a.size * a.dtype.itemsize for a in ins)
    return pl.pallas_call(
        kernel,
        in_specs=[in_vmem] * len(ins) + [anywhere] * len(ready),
        out_specs=[in_vmem] * len(outs),
        out_shape=[jax.ShapeDtypeStruct(tuple(shape), d) for *shape, d in outs],
        scratch_shapes=scratch,
        compiler_params=pltpu.CompilerParams(vmem_limit_bytes=16 << 20),
        cost_estimate=cost(us),
    )(*ins, *ready)


def lay_two(r0, r1, r2, r3, out, wide):
    for i, ref in enumerate((r0, r1, r2, r3)):
        wide[2 * i : 2 * i + 2] = ref[...].astype(f32)
    out[...] = wide[...].astype(bf16)


def lay(*refs):
    *ins, out = refs
    count = out.shape[0] // ins[0].shape[0]
    out[...] = jnp.concatenate([r[...].astype(f32) for r in ins[:count]], axis=0).astype(bf16)


def split_second(keep_a, r1, r2, r3, keep_b, rz, a1, b1, b2, b3, out_a, out_b):
    mine, other = [
        keep_a[:, i * 512 : (i + 1) * 512] + take(r1, i, 2) + take(r2, i, 2) + take(r3, i, 2)
        for i in range(2)
    ]
    out_a[...] = mine
    put(a1, [other], row_code(top_of([other])))
    low = [keep_b[:, d * 512 : (d + 1) * 512] + take(rz, d, 4) for d in range(4)]
    out_b[...] = low[0]
    code = row_code(top_of(low[1:]))
    for d, ref in ((1, b1), (2, b2), (3, b3)):
        put(ref, [low[d]], code)


def join_last(keep_a, rz, keep_b, r1, r2, r3, _, out_a, out_b):
    out_a[...] = keep_a[...] + take(rz, 0, 1)
    out_b[...] = keep_b[...] + take(r1, 0, 1) + take(r2, 0, 1) + take(r3, 0, 1)


def token_order(me):
    zl, x, zh, y, c = me
    r = lax.iota(jnp.int32, 256)
    t, i, j, dy, dx, k = r % 2, (r // 2) % 2, (r // 4) % 2, (r // 8) % 4, (r // 32) % 4, r // 128
    zl_, zh_, y_, x_, c_ = (zl + i) % 2, (zh + j) % 2, (y + dy) % 4, (x + dx) % 4, (c + k) % 2
    return ((((zl_ * 4 + x_) * 2 + zh_) * 4 + y_) * 2 + c_) * 2 + t


def gathered_order(me):
    zl, x, zh, y, c = me
    r = lax.iota(jnp.int32, 256)
    t, i, j, dy, dx, k = r % 2, (r // 2) % 2, (r // 4) % 2, (r // 8) % 4, (r // 32) % 4, r // 128
    zl_, zh_, y_, c_ = (zl + i) % 2, (zh + j) % 2, (y + dy) % 4, (c + k) % 2
    x_ = jnp.bitwise_xor(x, jnp.bitwise_xor(dx, dx // 2))
    return ((((zl_ * 4 + x_) * 2 + zh_) * 4 + y_) * 2 + c_) * 2 + t


def placing(order):
    n = order.shape[0]
    return (lax.broadcasted_iota(jnp.int32, (n, n), 0) == order[None, :]).astype(bf16)


def grad_rows(grad, head):
    feats, depth = head.shape
    steps = 8
    wide = feats // steps

    def kernel(grad_ref, head_ref, far_ref, near_ref, held, sems):
        copies = []
        for j in range(steps):
            part = head_ref.at[pl.ds(j * wide, wide), :]
            copies.append(pltpu.make_async_copy(part, held.at[j], sems.at[j]))
            copies[-1].start()
        for j in range(steps):
            copies[j].wait()
            both = lax.dot_general(
                grad_ref[...], held[j], (((1,), (1,)), ((), ())), preferred_element_type=f32
            )
            near_ref[:, j * wide : (j + 1) * wide] = both[:128]
            far_ref[:, j * wide : (j + 1) * wide] = both[128:]

    return pl.pallas_call(
        kernel,
        in_specs=[in_vmem, anywhere],
        out_specs=[in_vmem] * 2,
        out_shape=[jax.ShapeDtypeStruct((128, feats), f32)] * 2,
        scratch_shapes=[pltpu.VMEM((steps, wide, depth), bf16), pltpu.SemaphoreType.DMA((steps,))],
        compiler_params=pltpu.CompilerParams(vmem_limit_bytes=50 << 20),
        cost_estimate=cost(4),
    )(grad, head)


def scatter_rows(far, near):
    total = near + send((far * grad_scale).astype(f16), "c", 1).astype(f32) * (1.0 / grad_scale)
    out = (total * grad_scale).astype(f16).reshape(4, 32, -1)
    got = [send(out[d], "x", d) for d in (1, 2, 3)]
    total = total[:32] + sum(g.astype(f32) for g in got) * (1.0 / grad_scale)
    out = (total * grad_scale).astype(f16).reshape(4, 8, -1)
    got = [send(out[d], "y", d) for d in (1, 2, 3)]
    total = total[:8] + sum(g.astype(f32) for g in got) * (1.0 / grad_scale)
    across = ((1, ("zl",)), (2, ("zh",)), (3, ("zl", "zh")))
    return total[:2] + sum(cross_z(total[2 * i : 2 * i + 2], r) for i, r in across)


def body(teacher_hidden, teacher_head, student_hidden, student_head, targets):
    tokens = teacher_hidden.shape[0]
    vocab_dev = student_head.shape[1]
    me = tuple(lax.axis_index(a) for a in axes)
    zl, x, zh, y, c = me
    j = jnp.arange(8, dtype=jnp.int32)
    column = (((zh + j // 4) % 2) * 4 + (y + j % 4) % 4) * 2

    ring = [("zl",), ("zh",), ("zl", "zh")]
    rows = [student_hidden] + [cross_z(student_hidden, r) for r in ring]
    (rows,) = whole_call(lay_two, rows, [(8, 4096, bf16)], scratch=[pltpu.VMEM((8, 4096), f32)])
    rows = [rows] + [shift(rows, "y", i) for i in (1, 2, 3)]
    (rows,) = whole_call(lay, rows, [(32, 4096, bf16)], us=80)
    paired = lax.ppermute(rows, "x", ring_pair("x", True))
    other = far_products(teacher_hidden, teacher_head, column + 1 - c)
    other = send(other, "c", 1)
    first = first_products(teacher_hidden, teacher_head, column[:4] + c)
    a1, a2, a3, b1, keep_a, keep_b = own_products(
        teacher_hidden, teacher_head, column[4:] + c, first, other, [rows]
    )
    a1, a2, a3, b1 = send(a1, "y", 1), send(a2, "y", 2), send(a3, "y", 3), send(b1, "zh", 1)
    (rows,) = whole_call(lay, [rows, paired], [(64, 4096, bf16)], [keep_b])
    paired = lax.ppermute(rows, "x", ring_pair("x", False))
    a1, b1, b2, b3, keep_a, keep_b = whole_call(
        split_second,
        [keep_a, a1, a2, a3, keep_b, b1],
        [(128, 640, i16)] * 4 + [(128, 512, f32)] * 2,
    )
    a1, b1, b2, b3 = send(a1, "zh", 1), send(b1, "y", 1), send(b2, "y", 2), send(b3, "y", 3)

    (rows,) = whole_call(lay, [rows, paired], [(128, 4096, bf16)], [keep_a])
    gathered = jnp.concatenate([rows, shift(rows, "c", 1)], axis=0)
    place = placing(gathered_order(me))
    hidden_all = jnp.dot(place, gathered, preferred_element_type=f32).astype(bf16)
    logits_s = jnp.dot(hidden_all, student_head, preferred_element_type=f32)
    logits_t = whole_call(
        join_last, [keep_a, a1, keep_b, b1, b2, b3], [(128, 512, f32)] * 2, [logits_s]
    )
    logits_t = jnp.concatenate(logits_t, axis=0)

    offset = lax.axis_index(axes) * vocab_dev
    columns = offset + lax.broadcasted_iota(jnp.int32, (1, vocab_dev), 1)
    hit = (columns == targets[:, None]).astype(f32)
    top_t = jnp.max(logits_t, axis=1)
    exp_t = jnp.exp(logits_t - top_t[:, None])
    top_s = jnp.max(logits_s, axis=1)
    stats = jnp.stack(
        [
            top_t,
            jnp.sum(exp_t, axis=1),
            jnp.sum(exp_t * logits_s, axis=1),
            jnp.sum(exp_t * logits_t, axis=1),
            top_s,
            jnp.sum(jnp.exp(logits_s - top_s[:, None]), axis=1),
            jnp.sum(hit * logits_s, axis=1),
            jnp.zeros((tokens,), f32),
        ]
    )
    stats = merge_all(stats)
    norm_t = stats[0] + jnp.log(stats[1])
    norm_s = stats[4] + jnp.log(stats[5])
    mass = stats[1] / stats[1]
    cross = stats[2] / stats[1]
    entropy = stats[3] / stats[1] - mass * norm_t
    loss = jnp.sum(entropy - (cross - mass * norm_s) + ce_weight * (norm_s - stats[6])) / tokens

    probs = jnp.exp(logits_t - norm_t[:, None]).astype(bf16).astype(f32)
    probs_s = jnp.exp(logits_s - norm_s[:, None])
    grad_logits = ((mass + ce_weight)[:, None] * probs_s - probs - ce_weight * hit).astype(bf16)
    head_grad = lax.dot_general(
        hidden_all, grad_logits, (((0,), (0,)), ((), ())), preferred_element_type=f32
    ).astype(bf16)
    sorted_grad = lax.dot_general(
        placing(token_order(me)), grad_logits, (((0,), (0,)), ((), ())), preferred_element_type=f32
    ).astype(bf16)
    hidden_grad = scatter_rows(*grad_rows(sorted_grad, student_head))
    return (loss, head_grad, hidden_grad)


def solution(mesh):
    fine = Mesh(mesh.devices.reshape(sizes), axes)
    tt, sv = ("zl", "x"), ("zh", "y", "c")
    placed = (P(None, sv), P(sv, tt), P(axes, None), P(None, axes), P())
    return jax.shard_map(
        body,
        mesh=fine,
        in_specs=placed,
        out_specs=(P(), P(None, axes), P(axes, None)),
        check_vma=False,
    )
```

```python
import jax
import jax.numpy as jnp
from jax import lax
from jax.experimental import pallas as pl
from jax.experimental.pallas import tpu as pltpu
from jax.sharding import Mesh, PartitionSpec as P

ce_weight = 0.5
f16, f32, bf16, i16 = jnp.float16, jnp.float32, jnp.bfloat16, jnp.int16
axes = ("zl", "x", "zh", "y", "c")
sizes = (2, 4, 2, 4, 2)
grad_scale = 4096.0


def shift(value, axis, step):
    size = sizes[axes.index(axis)]
    return lax.ppermute(value, axis, [((i + step) % size, i) for i in range(size)])


def send(value, axis, step):
    size = sizes[axes.index(axis)]
    return lax.ppermute(value, axis, [(i, (i + step) % size) for i in range(size)])


def cross_z(value, across):
    pairs = [(i, i ^ (2 * ("zl" in across) + ("zh" in across))) for i in range(4)]
    return lax.ppermute(value, ("zl", "zh"), pairs)


def ring_pair(axis, first):
    return [(0, 1), (1, 0), (2, 3), (3, 2)] if first else [(0, 3), (3, 0), (1, 2), (2, 1)]


def merge(a, b):
    top_t = jnp.maximum(a[0], b[0])
    top_s = jnp.maximum(a[4], b[4])
    at, bt = jnp.exp(a[0] - top_t), jnp.exp(b[0] - top_t)
    as_, bs = jnp.exp(a[4] - top_s), jnp.exp(b[4] - top_s)
    return jnp.stack(
        [
            top_t,
            a[1] * at + b[1] * bt,
            a[2] * at + b[2] * bt,
            a[3] * at + b[3] * bt,
            top_s,
            a[5] * as_ + b[5] * bs,
            a[6] + b[6],
            a[7] + b[7],
        ]
    )


def merge_all(stats):
    stats = merge(stats, send(stats, "c", 1))
    for axis in ("x", "y"):
        for first in (True, False):
            stats = merge(stats, lax.ppermute(stats, axis, ring_pair(axis, first)))
    one, two, three = [cross_z(stats, r) for r in (("zl",), ("zh",), ("zl", "zh"))]
    return merge(merge(stats, one), merge(two, three))


def row_code(top):
    return jnp.ceil(8.0 * jnp.log2(jnp.maximum(top, 1e-30)) + 0.01)


def step_of(code):
    return jnp.exp2(code * 0.125) * (1.0 / 32000.0)


def top_of(blocks):
    top = jnp.max(jnp.abs(blocks[0]), axis=1, keepdims=True)
    for block in blocks[1:]:
        top = jnp.maximum(top, jnp.max(jnp.abs(block), axis=1, keepdims=True))
    return top


def put(ref, blocks, code):
    inverse = 1.0 / step_of(code)
    for i, block in enumerate(blocks):
        ref[:, i * 512 : (i + 1) * 512] = jnp.round(block * inverse).astype(i16)
    n = len(blocks) * 512
    ref[:, n : n + 128] = jnp.broadcast_to(code, (code.shape[0], 128)).astype(i16)


def pack(ref, blocks, code):
    inverse = 1.0 / step_of(code)
    for i, block in enumerate(blocks):
        whole = jnp.round(block * inverse).astype(i16)
        for g in range(4):
            at = (4 * i + g) * 128
            ref[at : at + 128] = whole[:, g * 128 : (g + 1) * 128]
    codes = jnp.transpose(jnp.broadcast_to(code, (128, 128)))
    ref[len(blocks) * 512 :] = codes[:16].astype(i16)


def unpack(ref):
    count = ref.shape[0] // 512
    codes = ref[count * 512 :].astype(f32)[:1]
    step = step_of(jnp.transpose(jnp.broadcast_to(codes, (128, 128)))[:, :1])
    blocks = []
    for i in range(count):
        tiles = [ref[(4 * i + g) * 128 : (4 * i + g + 1) * 128].astype(f32) * step for g in range(4)]
        blocks.append(jnp.concatenate(tiles, axis=1))
    return blocks


def take(ref, i, count):
    step = step_of(ref[:, count * 512 : count * 512 + 128].astype(f32)[:, :1])
    return ref[:, i * 512 : (i + 1) * 512].astype(f32) * step


def cost(us):
    return pl.CostEstimate(flops=int(us * 1e9), bytes_accessed=int(us * 2.5e6), transcendentals=0)


anywhere = pl.BlockSpec(memory_space=pl.ANY)
in_vmem = pl.BlockSpec(memory_space=pltpu.VMEM)
in_smem = pl.BlockSpec(memory_space=pltpu.SMEM)


def fetch_blocks(order_ref, hidden_ref, head_ref, rows, held, sems):
    count = held.shape[0]
    copies = []
    whole = pltpu.make_async_copy(hidden_ref, rows, sems.at[count])
    whole.start()
    for j in range(count):
        columns = pl.ds(pl.multiple_of(order_ref[j] * 512, 512), 512)
        copies.append(pltpu.make_async_copy(head_ref.at[:, columns], held.at[j], sems.at[j]))
        copies[-1].start()
    whole.wait()
    return copies


def far_products(hidden, head, order):
    count = order.shape[0]
    rows, depth = hidden.shape

    def kernel(order_ref, hidden_ref, head_ref, out_ref, rows_ref, held, sems):
        copies = fetch_blocks(order_ref, hidden_ref, head_ref, rows_ref, held, sems)
        for j in range(count):
            copies[j].wait()
            block = jnp.dot(rows_ref[...], held[j], preferred_element_type=f32)
            put(out_ref.at[j], [block], row_code(top_of([block])))

    return pl.pallas_call(
        kernel,
        in_specs=[in_smem, anywhere, anywhere],
        out_specs=in_vmem,
        out_shape=jax.ShapeDtypeStruct((count, rows, 640), i16),
        scratch_shapes=[
            pltpu.VMEM((rows, depth), bf16),
            pltpu.VMEM((count, depth, 512), bf16),
            pltpu.SemaphoreType.DMA((count + 1,)),
        ],
        compiler_params=pltpu.CompilerParams(vmem_limit_bytes=50 << 20),
        cost_estimate=cost(6),
    )(order, hidden, head)


def first_products(hidden, head, order):
    count = order.shape[0]
    rows, depth = hidden.shape

    def kernel(order_ref, hidden_ref, head_ref, out_ref, rows_ref, held, sems):
        copies = fetch_blocks(order_ref, hidden_ref, head_ref, rows_ref, held, sems)
        for j in range(count):
            copies[j].wait()
            out_ref[j] = jnp.dot(rows_ref[...], held[j], preferred_element_type=f32)

    return pl.pallas_call(
        kernel,
        in_specs=[in_smem, anywhere, anywhere],
        out_specs=in_vmem,
        out_shape=jax.ShapeDtypeStruct((count, rows, 512), f32),
        scratch_shapes=[
            pltpu.VMEM((rows, depth), bf16),
            pltpu.VMEM((count, depth, 512), bf16),
            pltpu.SemaphoreType.DMA((count + 1,)),
        ],
        compiler_params=pltpu.CompilerParams(vmem_limit_bytes=50 << 20),
        cost_estimate=cost(4),
    )(order, hidden, head)


def own_products(hidden, head, order, first, other, ready):
    rows, depth = hidden.shape
    half = rows // 2

    def kernel(order_ref, hidden_ref, head_ref, first_ref, other_ref, *refs):
        a1, a2, a3, b1, keep_a, keep_b, rows_ref, held, sums, sems = refs[len(ready) :]
        copies = fetch_blocks(order_ref, hidden_ref, head_ref, rows_ref, held, sems)
        up, low = jnp.zeros((half, 1), f32), jnp.zeros((half, 1), f32)
        for j in range(8):
            if j < 4:
                block = first_ref[j]
            else:
                copies[j - 4].wait()
                block = jnp.dot(rows_ref[...], held[j - 4], preferred_element_type=f32)
            block += take(other_ref.at[j], 0, 1)
            top = jnp.max(jnp.abs(block), axis=1, keepdims=True)
            if j % 4:
                sums[j, :half] = block[:half]
                up = jnp.maximum(up, top[:half])
            else:
                keep_a[:, j * 128 : j * 128 + 512] = block[:half]
            if j >= 4:
                sums[j, half:] = block[half:]
                low = jnp.maximum(low, top[half:])
            else:
                keep_b[:, j * 512 : j * 512 + 512] = block[half:]
        code = row_code(up)
        for d, ref in ((1, a1), (2, a2), (3, a3)):
            pack(ref, [sums[d, :half], sums[4 + d, :half]], code)
        pack(b1, [sums[4 + d, half:] for d in range(4)], row_code(low))

    outs = [(1040, 128, i16)] * 3 + [(2064, 128, i16), (half, 1024, f32), (half, 2048, f32)]
    return pl.pallas_call(
        kernel,
        in_specs=[in_smem, anywhere, anywhere, in_vmem, in_vmem] + [anywhere] * len(ready),
        out_specs=[in_vmem] * len(outs),
        out_shape=[jax.ShapeDtypeStruct((m, n), d) for m, n, d in outs],
        scratch_shapes=[
            pltpu.VMEM((rows, depth), bf16),
            pltpu.VMEM((4, depth, 512), bf16),
            pltpu.VMEM((8, rows, 512), f32),
            pltpu.SemaphoreType.DMA((5,)),
        ],
        compiler_params=pltpu.CompilerParams(vmem_limit_bytes=44 << 20),
        cost_estimate=cost(7),
    )(order, hidden, head, first, other, *ready)


def whole_call(kernel, ins, outs, ready=(), scratch=(), us=0.5):
    total = sum(a.size * a.dtype.itemsize for a in ins)
    return pl.pallas_call(
        kernel,
        in_specs=[in_vmem] * len(ins) + [anywhere] * len(ready),
        out_specs=[in_vmem] * len(outs),
        out_shape=[jax.ShapeDtypeStruct(tuple(shape), d) for *shape, d in outs],
        scratch_shapes=scratch,
        compiler_params=pltpu.CompilerParams(vmem_limit_bytes=16 << 20),
        cost_estimate=cost(us),
    )(*ins, *ready)


def lay_two(r0, r1, r2, r3, out, wide):
    for i, ref in enumerate((r0, r1, r2, r3)):
        wide[2 * i : 2 * i + 2] = ref[...].astype(f32)
    out[...] = wide[...].astype(bf16)


def lay(*refs):
    *ins, out = refs
    count = out.shape[0] // ins[0].shape[0]
    out[...] = jnp.concatenate([r[...].astype(f32) for r in ins[:count]], axis=0).astype(bf16)


def hand_on(value, *rest):
    rest[-1][...] = value[...]


def split_second(keep_a, r1, r2, r3, keep_b, rz, a1, b1, b2, b3, out_a, out_b):
    got = [unpack(r) for r in (r1, r2, r3)]
    mine, other = [
        keep_a[:, i * 512 : (i + 1) * 512] + got[0][i] + got[1][i] + got[2][i] for i in range(2)
    ]
    out_a[...] = mine
    pack(a1, [other], row_code(top_of([other])))
    low = [keep_b[:, d * 512 : (d + 1) * 512] + g for d, g in enumerate(unpack(rz))]
    out_b[...] = low[0]
    code = row_code(top_of(low[1:]))
    for d, ref in ((1, b1), (2, b2), (3, b3)):
        pack(ref, [low[d]], code)


def join_last(keep_a, rz, keep_b, r1, r2, r3, _, out_a, out_b):
    out_a[...] = keep_a[...] + unpack(rz)[0]
    out_b[...] = keep_b[...] + unpack(r1)[0] + unpack(r2)[0] + unpack(r3)[0]


def token_order(me):
    zl, x, zh, y, c = me
    r = lax.iota(jnp.int32, 256)
    t, i, j, dy, dx, k = r % 2, (r // 2) % 2, (r // 4) % 2, (r // 8) % 4, (r // 32) % 4, r // 128
    zl_, zh_, y_, x_, c_ = (zl + i) % 2, (zh + j) % 2, (y + dy) % 4, (x + dx) % 4, (c + k) % 2
    return ((((zl_ * 4 + x_) * 2 + zh_) * 4 + y_) * 2 + c_) * 2 + t


def gathered_order(me):
    zl, x, zh, y, c = me
    r = lax.iota(jnp.int32, 256)
    t, i, j, dy, dx, k = r % 2, (r // 2) % 2, (r // 4) % 2, (r // 8) % 4, (r // 32) % 4, r // 128
    zl_, zh_, y_, c_ = (zl + i) % 2, (zh + j) % 2, (y + dy) % 4, (c + k) % 2
    x_ = jnp.bitwise_xor(x, jnp.bitwise_xor(dx, dx // 2))
    return ((((zl_ * 4 + x_) * 2 + zh_) * 4 + y_) * 2 + c_) * 2 + t


def placing(order):
    n = order.shape[0]
    return (lax.broadcasted_iota(jnp.int32, (n, n), 0) == order[None, :]).astype(bf16)


def grad_rows(grad, turn, head):
    feats, depth = head.shape
    steps = 8
    wide = feats // steps

    def kernel(grad_ref, turn_ref, head_ref, far_ref, near_ref):
        rows = jnp.dot(turn_ref[...], grad_ref[...], preferred_element_type=f32).astype(bf16)
        for j in range(steps):
            at = slice(j * wide, (j + 1) * wide)
            both = lax.dot_general(
                rows, head_ref[at], (((1,), (1,)), ((), ())), preferred_element_type=f32
            )
            near_ref[:, at] = both[:128]
            far_ref[:, at] = both[128:]

    return pl.pallas_call(
        kernel,
        in_specs=[in_vmem] * 3,
        out_specs=[in_vmem] * 2,
        out_shape=[jax.ShapeDtypeStruct((128, feats), f32)] * 2,
        compiler_params=pltpu.CompilerParams(vmem_limit_bytes=24 << 20),
        cost_estimate=cost(3),
    )(grad, turn, head)


def scatter_rows(far, near, ready):
    total = near + send((far * grad_scale).astype(f16), "c", 1).astype(f32) * (1.0 / grad_scale)
    out = (total * grad_scale).astype(f16).reshape(4, 32, -1)
    got = [send(out[d], "x", d) for d in (2, 1, 3)]
    total = total[:32] + sum(g.astype(f32) for g in got) * (1.0 / grad_scale)
    out = (total * grad_scale).astype(f16).reshape(4, 8, -1)
    got = [send(out[d], "y", d) for d in (2, 1, 3)]
    (own,) = whole_call(hand_on, [total[:8]], [(8, total.shape[1], f32)], ready)
    total = own + sum(g.astype(f32) for g in got) * (1.0 / grad_scale)
    across = ((1, ("zl",)), (2, ("zh",)), (3, ("zl", "zh")))
    return total[:2] + sum(cross_z(total[2 * i : 2 * i + 2], r) for i, r in across)


def body(teacher_hidden, teacher_head, student_hidden, student_head, targets):
    tokens = teacher_hidden.shape[0]
    vocab_dev = student_head.shape[1]
    me = tuple(lax.axis_index(a) for a in axes)
    zl, x, zh, y, c = me
    j = jnp.arange(8, dtype=jnp.int32)
    column = (((zh + j // 4) % 2) * 4 + (y + j % 4) % 4) * 2

    ring = [("zl",), ("zh",), ("zl", "zh")]
    rows = [student_hidden] + [cross_z(student_hidden, r) for r in ring]
    (rows,) = whole_call(lay_two, rows, [(8, 4096, bf16)], scratch=[pltpu.VMEM((8, 4096), f32)])
    rows = [rows] + [shift(rows, "y", i) for i in (1, 2, 3)]
    (rows,) = whole_call(lay, rows, [(32, 4096, bf16)], us=80)
    paired = lax.ppermute(rows, "x", ring_pair("x", True))
    other = far_products(teacher_hidden, teacher_head, column + 1 - c)
    other = send(other, "c", 1)
    first = first_products(teacher_hidden, teacher_head, column[:4] + c)
    a1, a2, a3, b1, keep_a, keep_b = own_products(
        teacher_hidden, teacher_head, column[4:] + c, first, other, [rows]
    )
    a2, b1, a1, a3 = send(a2, "y", 2), send(b1, "zh", 1), send(a1, "y", 1), send(a3, "y", 3)
    (rows,) = whole_call(lay, [rows, paired], [(64, 4096, bf16)], [keep_b])
    paired = lax.ppermute(rows, "x", ring_pair("x", False))
    a1, b1, b2, b3, keep_a, keep_b = whole_call(
        split_second,
        [keep_a, a1, a2, a3, keep_b, b1],
        [(528, 128, i16)] * 4 + [(128, 512, f32)] * 2,
    )
    b2, a1, b1, b3 = send(b2, "y", 2), send(a1, "zh", 1), send(b1, "y", 1), send(b3, "y", 3)

    (rows,) = whole_call(lay, [rows, paired], [(128, 4096, bf16)], [keep_a])
    gathered = jnp.concatenate([rows, shift(rows, "c", 1)], axis=0)
    place = placing(gathered_order(me))
    hidden_all = jnp.dot(place, gathered, preferred_element_type=f32).astype(bf16)
    logits_s = jnp.dot(hidden_all, student_head, preferred_element_type=f32)
    logits_t = whole_call(
        join_last, [keep_a, a1, keep_b, b1, b2, b3], [(128, 512, f32)] * 2, [logits_s]
    )
    logits_t = jnp.concatenate(logits_t, axis=0)

    offset = lax.axis_index(axes) * vocab_dev
    columns = offset + lax.broadcasted_iota(jnp.int32, (1, vocab_dev), 1)
    hit = (columns == targets[:, None]).astype(f32)
    top_t = jnp.max(logits_t, axis=1)
    exp_t = jnp.exp(logits_t - top_t[:, None])
    top_s = jnp.max(logits_s, axis=1)
    stats = jnp.stack(
        [
            top_t,
            jnp.sum(exp_t, axis=1),
            jnp.sum(exp_t * logits_s, axis=1),
            jnp.sum(exp_t * logits_t, axis=1),
            top_s,
            jnp.sum(jnp.exp(logits_s - top_s[:, None]), axis=1),
            jnp.sum(hit * logits_s, axis=1),
            jnp.zeros((tokens,), f32),
        ]
    )
    stats = merge_all(stats)
    norm_t = stats[0] + jnp.log(stats[1])
    norm_s = stats[4] + jnp.log(stats[5])
    mass = stats[1] / stats[1]
    cross = stats[2] / stats[1]
    entropy = stats[3] / stats[1] - mass * norm_t
    loss = jnp.sum(entropy - (cross - mass * norm_s) + ce_weight * (norm_s - stats[6])) / tokens

    probs = jnp.exp(logits_t - norm_t[:, None]).astype(bf16).astype(f32)
    probs_s = jnp.exp(logits_s - norm_s[:, None])
    grad_logits = ((mass + ce_weight)[:, None] * probs_s - probs - ce_weight * hit).astype(bf16)
    head_grad = lax.dot_general(
        hidden_all, grad_logits, (((0,), (0,)), ((), ())), preferred_element_type=f32
    ).astype(bf16)
    turn = (token_order(me)[:, None] == lax.broadcasted_iota(jnp.int32, (1, tokens), 1)).astype(bf16)
    hidden_grad = scatter_rows(*grad_rows(grad_logits, turn, student_head), [head_grad])
    return (loss, head_grad, hidden_grad)


def solution(mesh):
    fine = Mesh(mesh.devices.reshape(sizes), axes)
    tt, sv = ("zl", "x"), ("zh", "y", "c")
    placed = (P(None, sv), P(sv, tt), P(axes, None), P(None, axes), P())
    return jax.shard_map(
        body,
        mesh=fine,
        in_specs=placed,
        out_specs=(P(), P(None, axes), P(axes, None)),
        check_vma=False,
    )
```
